32 devices in a mesh: row: 8 (over y, x, core), col: 4 (over z).
Axes of the slice: x: 2, y: 2, z: 4, core: 2. Of those that a mesh axis runs over, the one named last changes fastest.
Arguments:
- embeddings: float32 [4096, 256], P(('col', 'row')), may hold values from -6 to 6
- levels: int32 [4096], P('row'), may hold values from 0 to 7
Outputs:
- responsibility: float32 [4096, 4096], P('row', 'col')
- availability: float32 [4096, 4096], P('row', 'col')
The draws below stay inside these ranges and needn't reach their ends.
All inputs are finite; a program needn't handle non-finite values.
Results may differ from the reference program's by a relative error of at most 0.0003.
Values sent between devices are 32-bit elements; how exact they have to be, the bound alone decides.
A program may use at most 64 MiB of HBM per device.

```python
import jax
import jax.numpy as jnp
from jax import lax

D = 256
ROWS_DEV = 512
ITERS = 2
POINTS = 4096
N_ROW = 8


def with_ends(array, own_key, low, top_value):
    spot = [jax.random.randint(jax.random.fold_in(own_key, axis), (), 0, length) for axis, length in enumerate(array.shape)]
    main_axis = array.shape.index(max(array.shape))
    beside = spot[:main_axis] + [(spot[main_axis] + 1) % array.shape[main_axis]] + spot[main_axis + 1:]
    return array.at[tuple(spot)].set(low).at[tuple(beside)].set(top_value)


def block_levels(key, dims, split, smallest, top_value):
    def one(dim, blocks):
        draws = jax.random.uniform(jax.random.fold_in(jax.random.fold_in(key, 6), dim), (blocks,), jnp.float32, smallest / len(split), top_value / len(split))
        return jnp.repeat(jnp.exp(draws), dims[dim] // blocks).reshape((-1,) + (1,) * (len(dims) - dim - 1))

    level = one(*split[0])
    for cut in split[1:]:
        level = level * one(*cut)
    return level


def bell_draw(stream_key, dims, width, limit, split=(), kind=jnp.bfloat16):
    entries = width * jax.random.normal(stream_key, dims, jnp.float32)
    if split:
        entries = entries * block_levels(stream_key, dims, split, -0.22, 0.18)
    return jnp.clip(entries, -limit, limit).astype(kind)


def setup_inputs(seed: int = 0) -> dict:
    splits = jax.random.split(jax.random.key(seed), 3)
    embeddings = bell_draw(splits[0], (POINTS, D), 1.0, 6.0, ((0, 32),), jnp.float32)
    levels = with_ends(jax.random.randint(splits[1], (POINTS,), 0, 8), jax.random.fold_in(splits[1], 1), 0, 7).astype(jnp.int32)
    return {"embeddings": embeddings, "levels": levels}


lowest_value = -1e+30

def normalize(vectors):
    return vectors * lax.rsqrt(lax.optimization_barrier(jnp.sum(vectors * vectors, axis=1, keepdims=True)) + 1e-06)

def top_two(values):
    best_value = lax.optimization_barrier(jnp.max(values, axis=1, keepdims=True))
    tie_count = lax.optimization_barrier(jnp.sum(jnp.where(values == best_value, 1, 0), axis=1, keepdims=True))
    remainder = lax.optimization_barrier(jnp.max(jnp.where(values < best_value, values, lowest_value), axis=1, keepdims=True))
    return (best_value, jnp.where(tie_count > 1, best_value, remainder))

def reference(embeddings, levels):
    unit_points = normalize(embeddings)
    preference = 0.25 * levels.astype(jnp.float32) - 1.0
    block_ids = jnp.arange(N_ROW, dtype=jnp.int32)
    column_ids = jnp.arange(POINTS, dtype=jnp.int32)
    local_ids = jnp.arange(ROWS_DEV, dtype=jnp.int32)

    def mask_of(block):
        return (block * ROWS_DEV + local_ids)[:, None] == column_ids[None, :]

    def similar_block(block):
        start = block * ROWS_DEV
        row_points = lax.dynamic_slice_in_dim(unit_points, start, ROWS_DEV, 0)
        row_pref = lax.dynamic_slice_in_dim(preference, start, ROWS_DEV, 0)
        product = jnp.dot(row_points, unit_points.T, precision=lax.Precision.HIGHEST, preferred_element_type=jnp.float32)
        return jnp.where(mask_of(block), row_pref[:, None], product)
    similar = lax.map(similar_block, block_ids)
    responsibility = jnp.zeros_like(similar)
    availability = jnp.zeros_like(similar)
    for iteration in range(ITERS):

        def resp_block(inputs):
            sim_rows, avail_rows, resp_rows, block = inputs
            combined = avail_rows + sim_rows
            best_value, second_value = top_two(combined)
            fresh = sim_rows - jnp.where(combined >= best_value, second_value, best_value)
            updated = 0.5 * resp_rows + 0.5 * fresh
            diagonal_mask = mask_of(block)
            positive = lax.optimization_barrier(jnp.sum(jnp.where(diagonal_mask, 0.0, jnp.maximum(updated, 0.0)), axis=0))
            diag_part = lax.optimization_barrier(jnp.sum(jnp.where(diagonal_mask, updated, 0.0), axis=0))
            return (updated, positive, diag_part)
        responsibility, positive, diag_part = lax.map(resp_block, (similar, availability, responsibility, block_ids))
        column_positive = lax.optimization_barrier(jnp.sum(positive, axis=0))
        self_resp = lax.optimization_barrier(jnp.sum(diag_part, axis=0))

        def avail_block(inputs):
            avail_rows, resp_rows, block = inputs
            renewed = jnp.where(mask_of(block), column_positive[None, :], jnp.minimum(0.0, self_resp[None, :] + column_positive[None, :] - jnp.maximum(resp_rows, 0.0)))
            return 0.5 * avail_rows + 0.5 * renewed
        availability = lax.map(avail_block, (availability, responsibility, block_ids))
    return (responsibility.reshape(POINTS, POINTS), availability.reshape(POINTS, POINTS))
```

```python
import functools

import jax
import jax.numpy as jnp
from jax import lax
from jax.experimental import pallas as pl
from jax.experimental.pallas import tpu as pltpu
from jax.sharding import PartitionSpec as P

ITERS = 2
LANES = 128
STEP = 32
LOWEST = -1e30
MESH = pl.DeviceIdType.MESH


def kernel(
    n_row, n_col, emb, levels, resp_out, avail_out,
    cols, zbuf, rows, cols_cat, rows_cat, sim, resp, avail, best, second, tops, sums,
    zs, zr, cs, cr, fs, rs, rr, ts, tr, us, ur, outs, local,
):
    span, width = emb.shape
    row_count, col_count = sim.shape
    groups, chunks = row_count // LANES, col_count // LANES
    per = n_row // n_col
    r, c = lax.axis_index("row"), lax.axis_index("col")
    sibling = r + 1 - 2 * lax.rem(r, 2)

    def at_row(o):
        return lax.rem(r + o, n_row)

    def at_col(o):
        return lax.rem(c + o, n_col)

    barrier = pltpu.get_barrier_semaphore()
    for o in range(1, n_row):
        pl.semaphore_signal(barrier, inc=1, device_id=(at_row(o), c), device_id_type=MESH)
    for o in range(1, n_col):
        pl.semaphore_signal(barrier, inc=1, device_id=(r, at_col(o)), device_id_type=MESH)

    def part(index):
        return pl.ds(pl.multiple_of(index * span, span), span)

    own = emb[...]
    cols[part(r), :] = own * lax.rsqrt(jnp.sum(own * own, axis=1, keepdims=True) + 1e-06)
    pl.semaphore_wait(barrier, n_row + n_col - 2)

    def col_copy(block, send, target):
        return pltpu.make_async_remote_copy(
            src_ref=cols.at[part(block), :], dst_ref=cols.at[part(block), :],
            send_sem=send, recv_sem=cr.at[block], device_id=(target, c), device_id_type=MESH,
        )

    def z_copy(o, slot):
        return pltpu.make_async_remote_copy(
            src_ref=cols.at[part(r), :], dst_ref=zbuf.at[slot],
            send_sem=zs.at[o], recv_sem=zr.at[slot], device_id=(r, at_col(o)), device_id_type=MESH,
        )

    def row_copy(o, slot, place, target):
        return pltpu.make_async_remote_copy(
            src_ref=zbuf.at[slot], dst_ref=rows.at[part(place), :],
            send_sem=rs.at[o], recv_sem=rr.at[place], device_id=(target, c), device_id_type=MESH,
        )

    half = n_row // 2
    for o in range(1, n_col):
        z_copy(o, c).start()
    for o in range(1, half):
        col_copy(r, cs.at[o], at_row(2 * o)).start()
    col_copy(r, cs.at[0], sibling).start()

    place = lax.rem(r, n_col)

    def target_of(o):
        slot = at_col(n_col - o)
        return slot, slot * per + r // n_col

    for o in range(1, half):
        source = at_row(n_row - 2 * o)
        col_copy(source, fs.at[o], sibling).wait_recv()
        col_copy(source, fs.at[o], sibling).start()
    for o in range(1, n_col):
        slot, target = target_of(o)
        z_copy(o, slot).wait_recv()

        @pl.when(target != r)
        def _():
            row_copy(o, slot, place, target).start()

        @pl.when(target == r)
        def _():
            pltpu.make_async_copy(zbuf.at[slot], rows.at[part(place), :], local).start()
            pltpu.make_async_copy(zbuf.at[slot], rows.at[part(place), :], local).wait()

    col_copy(sibling, cs.at[0], sibling).wait_recv()
    for o in range(1, half):
        col_copy(lax.rem(sibling + n_row - 2 * o, n_row), fs.at[o], sibling).wait_recv()

    def split(ref):
        value = ref[...]
        high = value.astype(jnp.bfloat16)
        return high, (value - high.astype(jnp.float32)).astype(jnp.bfloat16)

    high, low = split(cols)
    cols_cat[:, :width] = high
    cols_cat[:, width : 2 * width] = low
    cols_cat[:, 2 * width :] = high

    source_col = r // per
    first = lax.rem(r, per) * n_col

    @pl.when(source_col == c)
    def _():
        for q in range(n_col):
            rows[q * span : (q + 1) * span, :] = cols[part(first + q), :]

    @pl.when(source_col != c)
    def _():
        for q in range(n_col):

            @pl.when(first + q != r)
            def _():
                row_copy(0, c, q, sibling).wait_recv()

    high, low = split(rows)
    rows_cat[:, :width] = high
    rows_cat[:, width : 2 * width] = high
    rows_cat[:, 2 * width :] = low

    wide = 2 * LANES

    @pl.loop(0, col_count // wide)
    def _(k):
        lanes = pl.ds(pl.multiple_of(k * wide, wide), wide)
        sim[:, lanes] = lax.dot_general(
            rows_cat[...], cols_cat[lanes, :], (((1,), (1,)), ((), ())),
            preferred_element_type=jnp.float32,
        )

    offset = r * row_count - c * col_count
    on_diagonal = (offset >= 0) & (offset < col_count)
    eye = lax.broadcasted_iota(jnp.int32, (LANES, LANES), 0) == lax.broadcasted_iota(
        jnp.int32, (LANES, LANES), 1
    )
    slant = lax.broadcasted_iota(jnp.int32, (STEP, LANES), 1) - lax.broadcasted_iota(
        jnp.int32, (STEP, LANES), 0
    )

    def tile_of(g):
        return (
            pl.ds(g * LANES, LANES),
            pl.ds(pl.multiple_of(offset + g * LANES, LANES), LANES),
        )

    @pl.when(on_diagonal)
    def _():
        preference = 0.25 * levels[...].astype(jnp.float32) - 1.0
        for g in range(groups):
            tile = tile_of(g)
            sim[tile] = jnp.where(eye, preference[g : g + 1, :], sim[tile])

    def spread(value):
        return jnp.broadcast_to(value, (value.shape[0], LANES))

    def lanes_of(k):
        return pl.ds(k * LANES, LANES)

    def rows_at(i):
        return pl.ds(pl.multiple_of(i * STEP, STEP), STEP)

    def top_pass(entry):
        @pl.loop(0, row_count // STEP)
        def _(i):
            here = rows_at(i)
            one = entry(i, here, 0)
            two = jnp.full_like(one, LOWEST)
            for k in range(1, chunks):
                value = entry(i, here, k)
                two = jnp.maximum(two, jnp.minimum(one, value))
                one = jnp.maximum(one, value)
            top = jnp.max(one, axis=1, keepdims=True)
            count = jnp.sum(jnp.where(one == top, 1.0, 0.0), axis=1, keepdims=True)
            rest = jnp.max(
                jnp.maximum(jnp.where(one < top, one, LOWEST), two), axis=1, keepdims=True
            )
            best[here, :] = spread(top)
            second[here, :] = spread(jnp.where(count > 1.0, top, rest))

    def top_exchange(turn):
        for g in range(groups):
            for ref, base in ((best, 0), (second, groups)):
                tops[turn, c, base + g : base + g + 1, :] = jnp.sum(
                    jnp.where(eye, ref[g * LANES : (g + 1) * LANES, :], 0.0), axis=0, keepdims=True
                )

        def copy(o, slot):
            return pltpu.make_async_remote_copy(
                src_ref=tops.at[turn, c], dst_ref=tops.at[turn, slot],
                send_sem=ts.at[turn, o], recv_sem=tr.at[turn, slot],
                device_id=(r, at_col(o)), device_id_type=MESH,
            )

        for o in range(1, n_col):
            copy(o, c).start()
        for o in range(1, n_col):
            copy(o, at_col(n_col - o)).wait_recv()
        one, two = tops[turn, 0, :groups, :], tops[turn, 0, groups:, :]
        for q in range(1, n_col):
            other, another = tops[turn, q, :groups, :], tops[turn, q, groups:, :]
            two = jnp.maximum(jnp.minimum(one, other), jnp.maximum(two, another))
            one = jnp.maximum(one, other)
        for g in range(groups):
            for ref, value in ((best, one), (second, two)):
                ref[g * LANES : (g + 1) * LANES, :] = spread(
                    jnp.sum(jnp.where(eye, value[g : g + 1, :], 0.0), axis=1, keepdims=True)
                )
        return lambda: [copy(o, c).wait_send() for o in range(1, n_col)]

    def resp_pass(turn):
        for k in range(chunks):
            lanes = lanes_of(k)

            def body(i, total):
                here = rows_at(i)
                similar = sim[here, lanes]
                combined = similar if turn == 0 else avail[here, lanes] + similar
                fresh = similar - jnp.where(combined >= best[here, :], second[here, :], best[here, :])
                updated = 0.5 * fresh if turn == 0 else 0.5 * resp[here, lanes] + 0.5 * fresh
                resp[here, lanes] = updated
                positive = jnp.where(
                    slant == offset + i * STEP - k * LANES, 0.0, jnp.maximum(updated, 0.0)
                )
                return total + jnp.sum(positive.reshape(STEP // 8, 8, LANES), axis=0)

            total = lax.fori_loop(
                0, row_count // STEP, body, jnp.zeros((8, LANES), jnp.float32), unroll=2
            )
            sums[turn, r, k : k + 1, :] = jnp.sum(total, axis=0, keepdims=True)
        sums[turn, r, chunks:, :] = jnp.zeros((chunks, LANES), jnp.float32)

        @pl.when(on_diagonal)
        def _():
            for g in range(groups):
                sums[turn, r, pl.ds(chunks + offset // LANES + g, 1), :] = jnp.sum(
                    jnp.where(eye, resp[tile_of(g)], 0.0), axis=0, keepdims=True
                )

    def sum_copy(turn, o, slot):
        return pltpu.make_async_remote_copy(
            src_ref=sums.at[turn, r], dst_ref=sums.at[turn, slot],
            send_sem=us.at[turn, o], recv_sem=ur.at[turn, slot],
            device_id=(at_row(o), c), device_id_type=MESH,
        )

    def sum_exchange(turn):
        for o in range(1, n_row):
            sum_copy(turn, o, r).start()
        for o in range(1, n_row):
            sum_copy(turn, o, at_row(n_row - o)).wait_recv()
        total = sums[turn, 0]
        for q in range(1, n_row):
            total = total + sums[turn, q]
        positive = total[:chunks, :]
        return positive, total[chunks:, :] + positive

    def renewed(stats, i, here, k):
        positive, both = stats
        return jnp.where(
            slant == offset + i * STEP - k * LANES,
            positive[k : k + 1, :],
            jnp.minimum(0.0, both[k : k + 1, :] - jnp.maximum(resp[here, lanes_of(k)], 0.0)),
        )

    top_pass(lambda i, here, k: sim[here, lanes_of(k)])
    tops_sent = [top_exchange(0)]
    resp_pass(0)
    stats = sum_exchange(0)

    def second_entry(i, here, k):
        value = 0.5 * renewed(stats, i, here, k)
        avail[here, lanes_of(k)] = value
        return value + sim[here, lanes_of(k)]

    top_pass(second_entry)
    tops_sent.append(top_exchange(1))
    resp_pass(1)
    resp_copy = pltpu.make_async_copy(resp, resp_out, local)
    for o in range(1, n_row):
        sum_copy(1, o, r).start()
    resp_copy.start()
    for o in range(1, n_row):
        sum_copy(1, o, at_row(n_row - o)).wait_recv()
    total = sums[1, 0]
    for q in range(1, n_row):
        total = total + sums[1, q]
    positive = total[:chunks, :]
    last = (positive, total[chunks:, :] + positive)

    def out_copy(g):
        piece = pl.ds(g * LANES, LANES)
        return pltpu.make_async_copy(avail.at[piece, :], avail_out.at[piece, :], outs.at[g])

    for g in range(groups):

        @pl.loop(g * (LANES // STEP), (g + 1) * (LANES // STEP))
        def _(i):
            here = rows_at(i)
            for k in range(chunks):
                lanes = lanes_of(k)
                avail[here, lanes] = 0.5 * avail[here, lanes] + 0.5 * renewed(last, i, here, k)

        out_copy(g).start()

    for o in range(1, n_col):
        z_copy(o, c).wait_send()
        slot, target = target_of(o)

        @pl.when(target != r)
        def _():
            row_copy(o, slot, place, target).wait_send()

    for o in range(1, half):
        col_copy(r, cs.at[o], at_row(2 * o)).wait_send()
        col_copy(at_row(n_row - 2 * o), fs.at[o], sibling).wait_send()
    col_copy(r, cs.at[0], sibling).wait_send()
    for sent in tops_sent:
        sent()
    for turn in range(ITERS):
        for o in range(1, n_row):
            sum_copy(turn, o, r).wait_send()
    resp_copy.wait()
    for g in range(groups):
        out_copy(g).wait()


def shards(embeddings, levels):
    n_row, n_col = lax.axis_size("row"), lax.axis_size("col")
    span, width = embeddings.shape
    row_count = levels.shape[0]
    col_count = span * n_row
    groups, chunks = row_count // LANES, col_count // LANES
    full = jax.ShapeDtypeStruct((row_count, col_count), jnp.float32)
    dma = pltpu.SemaphoreType.DMA
    return pl.pallas_call(
        functools.partial(kernel, n_row, n_col),
        out_shape=(full, full),
        in_specs=[pl.BlockSpec(memory_space=pltpu.VMEM)] * 2,
        out_specs=[pl.BlockSpec(memory_space=pl.ANY)] * 2,
        scratch_shapes=[
            pltpu.VMEM((col_count, width), jnp.float32),
            pltpu.VMEM((n_col, span, width), jnp.float32),
            pltpu.VMEM((row_count, width), jnp.float32),
            pltpu.VMEM((col_count, 3 * width), jnp.bfloat16),
            pltpu.VMEM((row_count, 3 * width), jnp.bfloat16),
            pltpu.VMEM((row_count, col_count), jnp.float32),
            pltpu.VMEM((row_count, col_count), jnp.float32),
            pltpu.VMEM((row_count, col_count), jnp.float32),
            pltpu.VMEM((row_count, LANES), jnp.float32),
            pltpu.VMEM((row_count, LANES), jnp.float32),
            pltpu.VMEM((ITERS, n_col, 2 * groups, LANES), jnp.float32),
            pltpu.VMEM((ITERS, n_row, 2 * chunks, LANES), jnp.float32),
            dma((n_col,)), dma((n_col,)),
            dma((n_row,)), dma((n_row,)), dma((n_row,)),
            dma((n_col,)), dma((n_col,)),
            dma((ITERS, n_col)), dma((ITERS, n_col)),
            dma((ITERS, n_row)), dma((ITERS, n_row)),
            dma((groups,)), dma,
        ],
        compiler_params=pltpu.CompilerParams(
            collective_id=0, has_side_effects=True, vmem_limit_bytes=58 * 1024 * 1024
        ),
        cost_estimate=pl.CostEstimate(
            flops=6 * row_count * col_count * width,
            bytes_accessed=8 * row_count * col_count,
            transcendentals=0,
        ),
    )(embeddings, levels.reshape(groups, LANES))


def solution(mesh):
    return jax.shard_map(
        shards,
        mesh=mesh,
        in_specs=(P(("col", "row"), None), P("row")),
        out_specs=(P("row", "col"), P("row", "col")),
        check_vma=False,
    )
```

```python
import functools

import jax
import jax.numpy as jnp
from jax import lax
from jax.experimental import pallas as pl
from jax.experimental.pallas import tpu as pltpu
from jax.sharding import PartitionSpec as P

ITERS = 2
LANES = 128
STEP = 32
LOWEST = -1e30
MESH = pl.DeviceIdType.MESH


def kernel(
    n_row, n_col, emb, levels, resp, avail, final,
    cols, zbuf, rows, cols_cat, rows_cat, sim, best, second, tops, sums,
    zs, zr, zd, cs, cr, fs, rs, rr, ts, tr, us, ur, local,
):
    span, width = emb.shape
    row_count, col_count = sim.shape
    groups, chunks = row_count // LANES, col_count // LANES
    per = n_row // n_col
    r, c = lax.axis_index("row"), lax.axis_index("col")
    sibling = r + 1 - 2 * lax.rem(r, 2)

    def at_row(o):
        return lax.rem(r + o, n_row)

    def at_col(o):
        return lax.rem(c + o, n_col)

    barrier = pltpu.get_barrier_semaphore()
    for o in range(1, n_row):
        pl.semaphore_signal(barrier, inc=1, device_id=(at_row(o), c), device_id_type=MESH)
    for o in range(1, n_col):
        pl.semaphore_signal(barrier, inc=1, device_id=(r, at_col(o)), device_id_type=MESH)

    def part(index):
        return pl.ds(pl.multiple_of(index * span, span), span)

    own = emb[...]
    cols[part(r), :] = own * lax.rsqrt(jnp.sum(own * own, axis=1, keepdims=True) + 1e-06)
    pl.semaphore_wait(barrier, n_row + n_col - 2)

    def col_copy(block, send, target):
        return pltpu.make_async_remote_copy(
            src_ref=cols.at[part(block), :], dst_ref=cols.at[part(block), :],
            send_sem=send, recv_sem=cr.at[block], device_id=(target, c), device_id_type=MESH,
        )

    def z_copy(source, send, slot, target):
        return pltpu.make_async_remote_copy(
            src_ref=source, dst_ref=zbuf.at[slot],
            send_sem=send, recv_sem=zr.at[slot], device_id=(r, target), device_id_type=MESH,
        )

    def row_copy(slot, place, target):
        return pltpu.make_async_remote_copy(
            src_ref=zbuf.at[slot], dst_ref=rows.at[part(place), :],
            send_sem=rs.at[slot], recv_sem=rr.at[place], device_id=(target, c), device_id_type=MESH,
        )

    half = n_row // 2
    mine = cols.at[part(r), :]
    place = lax.rem(r, n_col)

    def z_own(way):
        return z_copy(mine, zd.at[(way + 1) // 2], c, c + way)

    def z_pass(slot, way):
        return z_copy(zbuf.at[slot], zs.at[slot], slot, c + way)

    def inside(index):
        return (index >= 0) & (index < n_col)

    for way in (1, -1):

        @pl.when(inside(c + way))
        def _():
            z_own(way).start()

    for o in range(1, half):
        col_copy(r, cs.at[o], at_row(2 * o)).start()
    col_copy(r, cs.at[0], sibling).start()

    def col_step(o):
        source = at_row(n_row - 2 * o)
        col_copy(source, fs.at[o], sibling).wait_recv()
        col_copy(source, fs.at[o], sibling).start()

    for o in range(1, n_col):
        for way in (1, -1):
            slot = c - way * o

            @pl.when(inside(slot))
            def _():
                z_copy(mine, zs.at[slot], slot, c).wait_recv()

                @pl.when(inside(c + way))
                def _():
                    z_pass(slot, way).start()

                target = slot * per + r // n_col

                @pl.when(target != r)
                def _():
                    row_copy(slot, place, target).start()

                @pl.when(target == r)
                def _():
                    move = pltpu.make_async_copy(zbuf.at[slot], rows.at[part(place), :], local)
                    move.start()
                    move.wait()

        if o < half:
            col_step(o)
    for o in range(n_col, half):
        col_step(o)

    col_copy(sibling, cs.at[0], sibling).wait_recv()
    for o in range(1, half):
        col_copy(lax.rem(sibling + n_row - 2 * o, n_row), fs.at[o], sibling).wait_recv()

    def split(ref):
        value = ref[...]
        high = value.astype(jnp.bfloat16)
        return high, (value - high.astype(jnp.float32)).astype(jnp.bfloat16)

    high, low = split(cols)
    cols_cat[:, :width] = high
    cols_cat[:, width : 2 * width] = low
    cols_cat[:, 2 * width :] = high

    source_col = r // per
    first = lax.rem(r, per) * n_col

    @pl.when(source_col == c)
    def _():
        for q in range(n_col):
            rows[q * span : (q + 1) * span, :] = cols[part(first + q), :]

    @pl.when(source_col != c)
    def _():
        for q in range(n_col):

            @pl.when(first + q != r)
            def _():
                row_copy(c, q, sibling).wait_recv()

    high, low = split(rows)
    rows_cat[:, :width] = high
    rows_cat[:, width : 2 * width] = high
    rows_cat[:, 2 * width :] = low

    wide = 2 * LANES

    @pl.loop(0, col_count // wide)
    def _(k):
        lanes = pl.ds(pl.multiple_of(k * wide, wide), wide)
        sim[:, lanes] = lax.dot_general(
            rows_cat[...], cols_cat[lanes, :], (((1,), (1,)), ((), ())),
            preferred_element_type=jnp.float32,
        )

    offset = r * row_count - c * col_count
    on_diagonal = (offset >= 0) & (offset < col_count)
    eye = lax.broadcasted_iota(jnp.int32, (LANES, LANES), 0) == lax.broadcasted_iota(
        jnp.int32, (LANES, LANES), 1
    )
    slant = lax.broadcasted_iota(jnp.int32, (STEP, LANES), 1) - lax.broadcasted_iota(
        jnp.int32, (STEP, LANES), 0
    )

    def tile_of(g):
        return (
            pl.ds(g * LANES, LANES),
            pl.ds(pl.multiple_of(offset + g * LANES, LANES), LANES),
        )

    @pl.when(on_diagonal)
    def _():
        preference = 0.25 * levels[...].astype(jnp.float32) - 1.0
        for g in range(groups):
            tile = tile_of(g)
            sim[tile] = jnp.where(eye, preference[g : g + 1, :], sim[tile])

    def spread(value):
        return jnp.broadcast_to(value, (value.shape[0], LANES))

    def lanes_of(k):
        return pl.ds(k * LANES, LANES)

    def rows_at(i):
        return pl.ds(pl.multiple_of(i * STEP, STEP), STEP)

    def top_pass(entry):
        @pl.loop(0, row_count // STEP)
        def _(i):
            here = rows_at(i)
            one = entry(i, here, 0)
            two = jnp.full_like(one, LOWEST)
            for k in range(1, chunks):
                value = entry(i, here, k)
                two = jnp.maximum(two, jnp.minimum(one, value))
                one = jnp.maximum(one, value)
            top = jnp.max(one, axis=1, keepdims=True)
            count = jnp.sum(jnp.where(one == top, 1.0, 0.0), axis=1, keepdims=True)
            rest = jnp.max(
                jnp.maximum(jnp.where(one < top, one, LOWEST), two), axis=1, keepdims=True
            )
            best[here, :] = spread(top)
            second[here, :] = spread(jnp.where(count > 1.0, top, rest))

    def top_exchange(turn):
        for g in range(groups):
            for ref, base in ((best, 0), (second, groups)):
                tops[turn, c, base + g : base + g + 1, :] = jnp.sum(
                    jnp.where(eye, ref[g * LANES : (g + 1) * LANES, :], 0.0), axis=0, keepdims=True
                )

        def copy(o, slot):
            return pltpu.make_async_remote_copy(
                src_ref=tops.at[turn, c], dst_ref=tops.at[turn, slot],
                send_sem=ts.at[turn, o], recv_sem=tr.at[turn, slot],
                device_id=(r, at_col(o)), device_id_type=MESH,
            )

        for o in range(1, n_col):
            copy(o, c).start()
        for o in range(1, n_col):
            copy(o, at_col(n_col - o)).wait_recv()
        one, two = tops[turn, 0, :groups, :], tops[turn, 0, groups:, :]
        for q in range(1, n_col):
            other, another = tops[turn, q, :groups, :], tops[turn, q, groups:, :]
            two = jnp.maximum(jnp.minimum(one, other), jnp.maximum(two, another))
            one = jnp.maximum(one, other)
        for g in range(groups):
            for ref, value in ((best, one), (second, two)):
                ref[g * LANES : (g + 1) * LANES, :] = spread(
                    jnp.sum(jnp.where(eye, value[g : g + 1, :], 0.0), axis=1, keepdims=True)
                )
        return lambda: [copy(o, c).wait_send() for o in range(1, n_col)]

    def resp_pass(turn):
        for k in range(chunks):
            lanes = lanes_of(k)

            def body(i, total):
                here = rows_at(i)
                similar = sim[here, lanes]
                combined = similar if turn == 0 else avail[here, lanes] + similar
                fresh = similar - jnp.where(combined >= best[here, :], second[here, :], best[here, :])
                updated = 0.5 * fresh if turn == 0 else 0.5 * resp[here, lanes] + 0.5 * fresh
                resp[here, lanes] = updated
                positive = jnp.where(
                    slant == offset + i * STEP - k * LANES, 0.0, jnp.maximum(updated, 0.0)
                )
                return total + jnp.sum(positive.reshape(STEP // 8, 8, LANES), axis=0)

            total = lax.fori_loop(
                0, row_count // STEP, body, jnp.zeros((8, LANES), jnp.float32), unroll=2
            )
            sums[turn, r, k : k + 1, :] = jnp.sum(total, axis=0, keepdims=True)
        sums[turn, r, chunks:, :] = jnp.zeros((chunks, LANES), jnp.float32)

        @pl.when(on_diagonal)
        def _():
            for g in range(groups):
                sums[turn, r, pl.ds(chunks + offset // LANES + g, 1), :] = jnp.sum(
                    jnp.where(eye, resp[tile_of(g)], 0.0), axis=0, keepdims=True
                )

    def sum_copy(turn, o, slot):
        return pltpu.make_async_remote_copy(
            src_ref=sums.at[turn, r], dst_ref=sums.at[turn, slot],
            send_sem=us.at[turn, o], recv_sem=ur.at[turn, slot],
            device_id=(at_row(o), c), device_id_type=MESH,
        )

    def sum_exchange(turn):
        for o in range(1, n_row):
            sum_copy(turn, o, r).start()
        for o in range(1, n_row):
            sum_copy(turn, o, at_row(n_row - o)).wait_recv()
        total = sums[turn, 0]
        for q in range(1, n_row):
            total = total + sums[turn, q]
        positive = total[:chunks, :]
        return positive, total[chunks:, :] + positive

    def renewed(stats, i, here, k):
        positive, both = stats
        return jnp.where(
            slant == offset + i * STEP - k * LANES,
            positive[k : k + 1, :],
            jnp.minimum(0.0, both[k : k + 1, :] - jnp.maximum(resp[here, lanes_of(k)], 0.0)),
        )

    top_pass(lambda i, here, k: sim[here, lanes_of(k)])
    tops_sent = [top_exchange(0)]
    resp_pass(0)
    stats = sum_exchange(0)

    def second_entry(i, here, k):
        value = 0.5 * renewed(stats, i, here, k)
        avail[here, lanes_of(k)] = value
        return value + sim[here, lanes_of(k)]

    top_pass(second_entry)
    tops_sent.append(top_exchange(1))
    resp_pass(1)
    positive, both = sum_exchange(1)
    final[:chunks, :] = positive
    final[chunks:, :] = both

    for way in (1, -1):

        @pl.when(inside(c + way))
        def _():
            z_own(way).wait_send()

        for o in range(1, n_col):
            slot = c - way * o

            @pl.when(inside(slot))
            def _():
                @pl.when(inside(c + way))
                def _():
                    z_pass(slot, way).wait_send()

                target = slot * per + r // n_col

                @pl.when(target != r)
                def _():
                    row_copy(slot, place, target).wait_send()

    for o in range(1, half):
        col_copy(r, cs.at[o], at_row(2 * o)).wait_send()
        col_copy(at_row(n_row - 2 * o), fs.at[o], sibling).wait_send()
    col_copy(r, cs.at[0], sibling).wait_send()
    for sent in tops_sent:
        sent()
    for turn in range(ITERS):
        for o in range(1, n_row):
            sum_copy(turn, o, r).wait_send()


def shards(embeddings, levels):
    n_row, n_col = lax.axis_size("row"), lax.axis_size("col")
    span, width = embeddings.shape
    row_count = levels.shape[0]
    col_count = span * n_row
    groups, chunks = row_count // LANES, col_count // LANES
    full = pltpu.VMEM((row_count, col_count), jnp.float32)
    dma = pltpu.SemaphoreType.DMA
    scratch = 4 * row_count * col_count + 10 * (row_count + col_count) * width
    resp, avail, final = pl.pallas_call(
        functools.partial(kernel, n_row, n_col),
        out_shape=(full, full, pltpu.VMEM((2 * chunks, LANES), jnp.float32)),
        in_specs=[pl.BlockSpec(memory_space=pltpu.VMEM)] * 2,
        out_specs=[pl.BlockSpec(memory_space=pltpu.VMEM)] * 3,
        scratch_shapes=[
            pltpu.VMEM((col_count, width), jnp.float32),
            pltpu.VMEM((n_col, span, width), jnp.float32),
            pltpu.VMEM((row_count, width), jnp.float32),
            pltpu.VMEM((col_count, 3 * width), jnp.bfloat16),
            pltpu.VMEM((row_count, 3 * width), jnp.bfloat16),
            pltpu.VMEM((row_count, col_count), jnp.float32),
            pltpu.VMEM((row_count, LANES), jnp.float32),
            pltpu.VMEM((row_count, LANES), jnp.float32),
            pltpu.VMEM((ITERS, n_col, 2 * groups, LANES), jnp.float32),
            pltpu.VMEM((ITERS, n_row, 2 * chunks, LANES), jnp.float32),
            dma((n_col,)), dma((n_col,)), dma((2,)),
            dma((n_row,)), dma((n_row,)), dma((n_row,)),
            dma((n_col,)), dma((n_col,)),
            dma((ITERS, n_col)), dma((ITERS, n_col)),
            dma((ITERS, n_row)), dma((ITERS, n_row)),
            dma,
        ],
        compiler_params=pltpu.CompilerParams(
            collective_id=0, has_side_effects=True, vmem_limit_bytes=scratch + 12 * 1024 * 1024
        ),
        cost_estimate=pl.CostEstimate(
            flops=6 * row_count * col_count * width,
            bytes_accessed=8 * row_count * col_count,
            transcendentals=0,
        ),
    )(embeddings, levels.reshape(groups, LANES))
    row = lax.axis_index("row") * row_count + jnp.arange(row_count, dtype=jnp.int32)
    col = lax.axis_index("col") * col_count + jnp.arange(col_count, dtype=jnp.int32)
    positive = final[:chunks].reshape(1, col_count)
    both = final[chunks:].reshape(1, col_count)
    renewed = jnp.where(
        row[:, None] == col[None, :],
        positive,
        jnp.minimum(0.0, both - jnp.maximum(resp, 0.0)),
    )
    return resp, 0.5 * avail + 0.5 * renewed


def solution(mesh):
    return jax.shard_map(
        shards,
        mesh=mesh,
        in_specs=(P(("col", "row"), None), P("row")),
        out_specs=(P("row", "col"), P("row", "col")),
        check_vma=False,
    )
```

```python
import functools

import jax
import jax.numpy as jnp
from jax import lax
from jax.experimental import pallas as pl
from jax.experimental.pallas import tpu as pltpu
from jax.sharding import PartitionSpec as P

ITERS = 2
LANES = 128
STEP = 32
PIECES = 2
LOWEST = -1e30
MESH = pl.DeviceIdType.MESH


def kernel(
    n_row, n_col, emb_hbm, levels_hbm, resp, avail, final,
    emb, levels, cols, zbuf, rows, cols_cat, rows_cat, sim, best, second, tops, sums,
    zs, zr, zd, cs, cr, fs, rs, rr, ts, tr, us, ur, local, entry,
):
    span, width = emb.shape
    row_count, col_count = sim.shape
    groups, chunks = row_count // LANES, col_count // LANES
    per = n_row // n_col
    r, c = lax.axis_index("row"), lax.axis_index("col")
    sibling = r + 1 - 2 * lax.rem(r, 2)

    def at_row(o):
        return lax.rem(r + o, n_row)

    def at_col(o):
        return lax.rem(c + o, n_col)

    emb_copy = pltpu.make_async_copy(emb_hbm, emb, entry.at[0])
    levels_copy = pltpu.make_async_copy(levels_hbm, levels, entry.at[1])
    emb_copy.start()
    levels_copy.start()
    barrier = pltpu.get_barrier_semaphore()
    for o in range(1, n_row):
        pl.semaphore_signal(barrier, inc=1, device_id=(at_row(o), c), device_id_type=MESH)
    for o in range(1, n_col):
        pl.semaphore_signal(barrier, inc=1, device_id=(r, at_col(o)), device_id_type=MESH)

    def part(index):
        return pl.ds(pl.multiple_of(index * span, span), span)

    emb_copy.wait()
    own = emb[...]
    cols[part(r), :] = own * lax.rsqrt(jnp.sum(own * own, axis=1, keepdims=True) + 1e-06)
    levels_copy.wait()
    pl.semaphore_wait(barrier, n_row + n_col - 2)

    def col_copy(block, send, target):
        return pltpu.make_async_remote_copy(
            src_ref=cols.at[part(block), :], dst_ref=cols.at[part(block), :],
            send_sem=send, recv_sem=cr.at[block], device_id=(target, c), device_id_type=MESH,
        )

    piece = span // PIECES

    def z_copy(source, send, slot, h, target):
        return pltpu.make_async_remote_copy(
            src_ref=source, dst_ref=zbuf.at[slot, pl.ds(h * piece, piece)],
            send_sem=send, recv_sem=zr.at[slot, h], device_id=(r, target), device_id_type=MESH,
        )

    def row_part(place, h):
        return pl.ds(pl.multiple_of(place * span + h * piece, piece), piece)

    def row_copy(slot, place, h, target):
        return pltpu.make_async_remote_copy(
            src_ref=zbuf.at[slot, pl.ds(h * piece, piece)], dst_ref=rows.at[row_part(place, h), :],
            send_sem=rs.at[slot, h], recv_sem=rr.at[place, h],
            device_id=(target, c), device_id_type=MESH,
        )

    half = n_row // 2
    place = lax.rem(r, n_col)

    def z_own(way, h):
        return z_copy(cols.at[row_part(r, h), :], zd.at[(way + 1) // 2, h], c, h, c + way)

    def z_pass(slot, way, h):
        return z_copy(zbuf.at[slot, pl.ds(h * piece, piece)], zs.at[slot, h], slot, h, c + way)

    def inside(index):
        return (index >= 0) & (index < n_col)

    for way in (1, -1):

        @pl.when(inside(c + way))
        def _():
            for h in range(PIECES):
                z_own(way, h).start()

    for o in range(1, half):
        col_copy(r, cs.at[o], at_row(2 * o)).start()
    col_copy(r, cs.at[0], sibling).start()

    def col_step(o):
        source = at_row(n_row - 2 * o)
        col_copy(source, fs.at[o], sibling).wait_recv()
        col_copy(source, fs.at[o], sibling).start()

    for o in range(1, n_col):
        for h in range(PIECES):
            for way in (1, -1):
                slot = c - way * o

                @pl.when(inside(slot))
                def _():
                    z_copy(cols.at[row_part(r, h), :], zs.at[slot, h], slot, h, c).wait_recv()

                    @pl.when(inside(c + way))
                    def _():
                        z_pass(slot, way, h).start()

                    target = slot * per + r // n_col

                    @pl.when(target != r)
                    def _():
                        row_copy(slot, place, h, target).start()

                    @pl.when(target == r)
                    def _():
                        move = pltpu.make_async_copy(
                            zbuf.at[slot, pl.ds(h * piece, piece)],
                            rows.at[row_part(place, h), :],
                            local,
                        )
                        move.start()
                        move.wait()

        if o < half:
            col_step(o)
    for o in range(n_col, half):
        col_step(o)

    col_copy(sibling, cs.at[0], sibling).wait_recv()
    for o in range(1, half):
        col_copy(lax.rem(sibling + n_row - 2 * o, n_row), fs.at[o], sibling).wait_recv()

    def split(ref):
        value = ref[...]
        high = value.astype(jnp.bfloat16)
        return high, (value - high.astype(jnp.float32)).astype(jnp.bfloat16)

    high, low = split(cols)
    cols_cat[:, :width] = high
    cols_cat[:, width : 2 * width] = low
    cols_cat[:, 2 * width :] = high

    source_col = r // per
    first = lax.rem(r, per) * n_col

    @pl.when(source_col == c)
    def _():
        for q in range(n_col):
            rows[q * span : (q + 1) * span, :] = cols[part(first + q), :]

    @pl.when(source_col != c)
    def _():
        for q in range(n_col):

            @pl.when(first + q != r)
            def _():
                for h in range(PIECES):
                    row_copy(c, q, h, sibling).wait_recv()

    high, low = split(rows)
    rows_cat[:, :width] = high
    rows_cat[:, width : 2 * width] = high
    rows_cat[:, 2 * width :] = low

    wide = 2 * LANES

    @pl.loop(0, col_count // wide)
    def _(k):
        lanes = pl.ds(pl.multiple_of(k * wide, wide), wide)
        sim[:, lanes] = lax.dot_general(
            rows_cat[...], cols_cat[lanes, :], (((1,), (1,)), ((), ())),
            preferred_element_type=jnp.float32,
        )

    offset = r * row_count - c * col_count
    on_diagonal = (offset >= 0) & (offset < col_count)
    eye = lax.broadcasted_iota(jnp.int32, (LANES, LANES), 0) == lax.broadcasted_iota(
        jnp.int32, (LANES, LANES), 1
    )
    slant = lax.broadcasted_iota(jnp.int32, (STEP, LANES), 1) - lax.broadcasted_iota(
        jnp.int32, (STEP, LANES), 0
    )

    def tile_of(g):
        return (
            pl.ds(g * LANES, LANES),
            pl.ds(pl.multiple_of(offset + g * LANES, LANES), LANES),
        )

    @pl.when(on_diagonal)
    def _():
        preference = 0.25 * levels[...].astype(jnp.float32) - 1.0
        for g in range(groups):
            tile = tile_of(g)
            sim[tile] = jnp.where(eye, preference[g : g + 1, :], sim[tile])

    def lanes_of(k):
        return pl.ds(k * LANES, LANES)

    def rows_at(i):
        return pl.ds(pl.multiple_of(i * STEP, STEP), STEP)

    def top_pass(entry):
        @pl.loop(0, row_count // STEP)
        def _(i):
            here = rows_at(i)
            one = entry(i, here, 0)
            two = jnp.full_like(one, LOWEST)
            for k in range(1, chunks):
                value = entry(i, here, k)
                two = jnp.maximum(two, jnp.minimum(one, value))
                one = jnp.maximum(one, value)
            best[here, :] = one
            second[here, :] = two

    def top_exchange(turn):
        for g in range(groups):
            tile = slice(g * LANES, (g + 1) * LANES)
            one, two = best[tile, :].T, second[tile, :].T
            top = jnp.max(one, axis=0, keepdims=True)
            count = jnp.sum(jnp.where(one == top, 1.0, 0.0), axis=0, keepdims=True)
            rest = jnp.max(
                jnp.maximum(jnp.where(one < top, one, LOWEST), two), axis=0, keepdims=True
            )
            tops[turn, c, g : g + 1, :] = top
            tops[turn, c, groups + g : groups + g + 1, :] = jnp.where(count > 1.0, top, rest)

        def copy(o, slot):
            return pltpu.make_async_remote_copy(
                src_ref=tops.at[turn, c], dst_ref=tops.at[turn, slot],
                send_sem=ts.at[turn, o], recv_sem=tr.at[turn, slot],
                device_id=(r, at_col(o)), device_id_type=MESH,
            )

        for o in range(1, n_col):
            copy(o, c).start()
        for o in range(1, n_col):
            copy(o, at_col(n_col - o)).wait_recv()
        one, two = tops[turn, 0, :groups, :], tops[turn, 0, groups:, :]
        for q in range(1, n_col):
            other, another = tops[turn, q, :groups, :], tops[turn, q, groups:, :]
            two = jnp.maximum(jnp.minimum(one, other), jnp.maximum(two, another))
            one = jnp.maximum(one, other)
        for g in range(groups):
            for ref, value in ((best, one), (second, two)):
                ref[g * LANES : (g + 1) * LANES, :] = jnp.broadcast_to(
                    value[g : g + 1, :], (LANES, LANES)
                ).T
        return lambda: [copy(o, c).wait_send() for o in range(1, n_col)]

    def resp_pass(turn):
        for k in range(chunks):
            lanes = lanes_of(k)

            def body(i, total):
                here = rows_at(i)
                similar = sim[here, lanes]
                combined = similar if turn == 0 else avail[here, lanes] + similar
                fresh = similar - jnp.where(combined >= best[here, :], second[here, :], best[here, :])
                updated = 0.5 * fresh if turn == 0 else 0.5 * resp[here, lanes] + 0.5 * fresh
                resp[here, lanes] = updated
                positive = jnp.where(
                    slant == offset + i * STEP - k * LANES, 0.0, jnp.maximum(updated, 0.0)
                )
                return total + jnp.sum(positive.reshape(STEP // 8, 8, LANES), axis=0)

            total = lax.fori_loop(
                0, row_count // STEP, body, jnp.zeros((8, LANES), jnp.float32), unroll=2
            )
            sums[turn, r, k : k + 1, :] = jnp.sum(total, axis=0, keepdims=True)
        sums[turn, r, chunks:, :] = jnp.zeros((chunks, LANES), jnp.float32)

        @pl.when(on_diagonal)
        def _():
            for g in range(groups):
                sums[turn, r, pl.ds(chunks + offset // LANES + g, 1), :] = jnp.sum(
                    jnp.where(eye, resp[tile_of(g)], 0.0), axis=0, keepdims=True
                )

    def sum_copy(turn, o, slot):
        return pltpu.make_async_remote_copy(
            src_ref=sums.at[turn, r], dst_ref=sums.at[turn, slot],
            send_sem=us.at[turn, o], recv_sem=ur.at[turn, slot],
            device_id=(at_row(o), c), device_id_type=MESH,
        )

    def sum_exchange(turn):
        for o in range(1, n_row):
            sum_copy(turn, o, r).start()
        for o in range(1, n_row):
            sum_copy(turn, o, at_row(n_row - o)).wait_recv()
        total = sums[turn, 0]
        for q in range(1, n_row):
            total = total + sums[turn, q]
        positive = total[:chunks, :]
        return positive, total[chunks:, :] + positive

    def renewed(stats, i, here, k):
        positive, both = stats
        return jnp.where(
            slant == offset + i * STEP - k * LANES,
            positive[k : k + 1, :],
            jnp.minimum(0.0, both[k : k + 1, :] - jnp.maximum(resp[here, lanes_of(k)], 0.0)),
        )

    top_pass(lambda i, here, k: sim[here, lanes_of(k)])
    tops_sent = [top_exchange(0)]
    resp_pass(0)
    stats = sum_exchange(0)

    def second_entry(i, here, k):
        value = 0.5 * renewed(stats, i, here, k)
        avail[here, lanes_of(k)] = value
        return value + sim[here, lanes_of(k)]

    top_pass(second_entry)
    tops_sent.append(top_exchange(1))
    resp_pass(1)
    positive, both = sum_exchange(1)
    final[:chunks, :] = positive
    final[chunks:, :] = both

    for way in (1, -1):

        @pl.when(inside(c + way))
        def _():
            for h in range(PIECES):
                z_own(way, h).wait_send()

        for o in range(1, n_col):
            slot = c - way * o

            @pl.when(inside(slot))
            def _():
                @pl.when(inside(c + way))
                def _():
                    for h in range(PIECES):
                        z_pass(slot, way, h).wait_send()

                target = slot * per + r // n_col

                @pl.when(target != r)
                def _():
                    for h in range(PIECES):
                        row_copy(slot, place, h, target).wait_send()

    for o in range(1, half):
        col_copy(r, cs.at[o], at_row(2 * o)).wait_send()
        col_copy(at_row(n_row - 2 * o), fs.at[o], sibling).wait_send()
    col_copy(r, cs.at[0], sibling).wait_send()
    for sent in tops_sent:
        sent()
    for turn in range(ITERS):
        for o in range(1, n_row):
            sum_copy(turn, o, r).wait_send()


def shards(embeddings, levels):
    n_row, n_col = lax.axis_size("row"), lax.axis_size("col")
    span, width = embeddings.shape
    row_count = levels.shape[0]
    col_count = span * n_row
    groups, chunks = row_count // LANES, col_count // LANES
    full = pltpu.VMEM((row_count, col_count), jnp.float32)
    dma = pltpu.SemaphoreType.DMA
    scratch = 4 * row_count * col_count + 10 * (row_count + col_count) * width
    resp, avail, final = pl.pallas_call(
        functools.partial(kernel, n_row, n_col),
        out_shape=(full, full, pltpu.VMEM((2 * chunks, LANES), jnp.float32)),
        in_specs=[pl.BlockSpec(memory_space=pltpu.HBM)] * 2,
        out_specs=[pl.BlockSpec(memory_space=pltpu.VMEM)] * 3,
        scratch_shapes=[
            pltpu.VMEM((span, width), jnp.float32),
            pltpu.VMEM((groups, LANES), jnp.int32),
            pltpu.VMEM((col_count, width), jnp.float32),
            pltpu.VMEM((n_col, span, width), jnp.float32),
            pltpu.VMEM((row_count, width), jnp.float32),
            pltpu.VMEM((col_count, 3 * width), jnp.bfloat16),
            pltpu.VMEM((row_count, 3 * width), jnp.bfloat16),
            pltpu.VMEM((row_count, col_count), jnp.float32),
            pltpu.VMEM((row_count, LANES), jnp.float32),
            pltpu.VMEM((row_count, LANES), jnp.float32),
            pltpu.VMEM((ITERS, n_col, 2 * groups, LANES), jnp.float32),
            pltpu.VMEM((ITERS, n_row, 2 * chunks, LANES), jnp.float32),
            dma((n_col, PIECES)), dma((n_col, PIECES)), dma((2, PIECES)),
            dma((n_row,)), dma((n_row,)), dma((n_row,)),
            dma((n_col, PIECES)), dma((n_col, PIECES)),
            dma((ITERS, n_col)), dma((ITERS, n_col)),
            dma((ITERS, n_row)), dma((ITERS, n_row)),
            dma, dma((2,)),
        ],
        compiler_params=pltpu.CompilerParams(
            collective_id=0, has_side_effects=True, vmem_limit_bytes=scratch + 12 * 1024 * 1024
        ),
        cost_estimate=pl.CostEstimate(
            flops=6 * row_count * col_count * width,
            bytes_accessed=8 * row_count * col_count,
            transcendentals=0,
        ),
    )(embeddings, levels.reshape(groups, LANES))
    row = lax.axis_index("row") * row_count + jnp.arange(row_count, dtype=jnp.int32)
    col = lax.axis_index("col") * col_count + jnp.arange(col_count, dtype=jnp.int32)
    positive = final[:chunks].reshape(1, col_count)
    both = final[chunks:].reshape(1, col_count)
    renewed = jnp.where(
        row[:, None] == col[None, :],
        positive,
        jnp.minimum(0.0, both - jnp.maximum(resp, 0.0)),
    )
    return resp, 0.5 * avail + 0.5 * renewed


def solution(mesh):
    return jax.shard_map(
        shards,
        mesh=mesh,
        in_specs=(P(("col", "row"), None), P("row")),
        out_specs=(P("row", "col"), P("row", "col")),
        check_vma=False,
    )
```

```python
import functools

import jax
import jax.numpy as jnp
from jax import lax
from jax.experimental import pallas as pl
from jax.experimental.pallas import tpu as pltpu
from jax.sharding import PartitionSpec as P

ITERS = 2
LANES = 128
STEP = 32
PIECES = 4
LOWEST = -1e30
MESH = pl.DeviceIdType.MESH


def kernel(
    n_row, n_col, emb_hbm, levels_hbm, resp, avail, final,
    emb, levels, cols, zbuf, rows, cols_cat, rows_cat, sim, best, second, tops, sums,
    zs, zr, zd, cs, cr, fs, rs, rr, ts, tr, us, ur, local, entry,
):
    span, width = emb.shape
    row_count, col_count = sim.shape
    groups, chunks = row_count // LANES, col_count // LANES
    per = n_row // n_col
    r, c = lax.axis_index("row"), lax.axis_index("col")
    sibling = r + 1 - 2 * lax.rem(r, 2)

    def at_row(o):
        return lax.rem(r + o, n_row)

    def at_col(o):
        return lax.rem(c + o, n_col)

    emb_copy = pltpu.make_async_copy(emb_hbm, emb, entry.at[0])
    levels_copy = pltpu.make_async_copy(levels_hbm, levels, entry.at[1])
    emb_copy.start()
    levels_copy.start()
    barrier = pltpu.get_barrier_semaphore()
    for o in range(1, n_row):
        pl.semaphore_signal(barrier, inc=1, device_id=(at_row(o), c), device_id_type=MESH)
    for o in range(1, n_col):
        pl.semaphore_signal(barrier, inc=1, device_id=(r, at_col(o)), device_id_type=MESH)

    def part(index):
        return pl.ds(pl.multiple_of(index * span, span), span)

    emb_copy.wait()
    own = emb[...]
    cols[part(r), :] = own * lax.rsqrt(jnp.sum(own * own, axis=1, keepdims=True) + 1e-06)
    levels_copy.wait()
    pl.semaphore_wait(barrier, n_row + n_col - 2)

    def col_copy(block, send, target):
        return pltpu.make_async_remote_copy(
            src_ref=cols.at[part(block), :], dst_ref=cols.at[part(block), :],
            send_sem=send, recv_sem=cr.at[block], device_id=(target, c), device_id_type=MESH,
        )

    piece = span // PIECES

    def z_copy(source, send, slot, h, target):
        return pltpu.make_async_remote_copy(
            src_ref=source, dst_ref=zbuf.at[slot, pl.ds(h * piece, piece)],
            send_sem=send, recv_sem=zr.at[slot, h], device_id=(r, target), device_id_type=MESH,
        )

    def row_part(place, h):
        return pl.ds(pl.multiple_of(place * span + h * piece, piece), piece)

    def row_copy(slot, place, h, target):
        return pltpu.make_async_remote_copy(
            src_ref=zbuf.at[slot, pl.ds(h * piece, piece)], dst_ref=rows.at[row_part(place, h), :],
            send_sem=rs.at[slot, h], recv_sem=rr.at[place, h],
            device_id=(target, c), device_id_type=MESH,
        )

    half = n_row // 2
    place = lax.rem(r, n_col)

    def z_own(way, h):
        return z_copy(cols.at[row_part(r, h), :], zd.at[(way + 1) // 2, h], c, h, c + way)

    def z_pass(slot, way, h):
        return z_copy(zbuf.at[slot, pl.ds(h * piece, piece)], zs.at[slot, h], slot, h, c + way)

    def inside(index):
        return (index >= 0) & (index < n_col)

    for way in (1, -1):

        @pl.when(inside(c + way))
        def _():
            for h in range(PIECES):
                z_own(way, h).start()

    for o in range(1, half):
        col_copy(r, cs.at[o], at_row(2 * o)).start()
    col_copy(r, cs.at[0], sibling).start()

    def col_step(o):
        source = at_row(n_row - 2 * o)
        col_copy(source, fs.at[o], sibling).wait_recv()
        col_copy(source, fs.at[o], sibling).start()

    for o in range(1, n_col):
        for h in range(PIECES):
            for way in (1, -1):
                slot = c - way * o

                @pl.when(inside(slot))
                def _():
                    z_copy(cols.at[row_part(r, h), :], zs.at[slot, h], slot, h, c).wait_recv()

                    @pl.when(inside(c + way))
                    def _():
                        z_pass(slot, way, h).start()

                    target = slot * per + r // n_col

                    @pl.when(target != r)
                    def _():
                        row_copy(slot, place, h, target).start()

                    @pl.when(target == r)
                    def _():
                        move = pltpu.make_async_copy(
                            zbuf.at[slot, pl.ds(h * piece, piece)],
                            rows.at[row_part(place, h), :],
                            local,
                        )
                        move.start()
                        move.wait()

        if o < half:
            col_step(o)
    for o in range(n_col, half):
        col_step(o)

    col_copy(sibling, cs.at[0], sibling).wait_recv()
    for o in range(1, half):
        col_copy(lax.rem(sibling + n_row - 2 * o, n_row), fs.at[o], sibling).wait_recv()

    def split(ref):
        value = ref[...]
        high = value.astype(jnp.bfloat16)
        return high, (value - high.astype(jnp.float32)).astype(jnp.bfloat16)

    high, low = split(cols)
    cols_cat[:, :width] = high
    cols_cat[:, width : 2 * width] = low
    cols_cat[:, 2 * width :] = high

    source_col = r // per
    first = lax.rem(r, per) * n_col

    @pl.when(source_col == c)
    def _():
        for q in range(n_col):
            rows[q * span : (q + 1) * span, :] = cols[part(first + q), :]

    @pl.when(source_col != c)
    def _():
        for q in range(n_col):

            @pl.when(first + q != r)
            def _():
                for h in range(PIECES):
                    row_copy(c, q, h, sibling).wait_recv()

    high, low = split(rows)
    rows_cat[:, :width] = high
    rows_cat[:, width : 2 * width] = high
    rows_cat[:, 2 * width :] = low

    wide = 2 * LANES

    @pl.loop(0, col_count // wide)
    def _(k):
        lanes = pl.ds(pl.multiple_of(k * wide, wide), wide)
        sim[:, lanes] = lax.dot_general(
            rows_cat[...], cols_cat[lanes, :], (((1,), (1,)), ((), ())),
            preferred_element_type=jnp.float32,
        )

    offset = r * row_count - c * col_count
    on_diagonal = (offset >= 0) & (offset < col_count)
    eye = lax.broadcasted_iota(jnp.int32, (LANES, LANES), 0) == lax.broadcasted_iota(
        jnp.int32, (LANES, LANES), 1
    )
    slant = lax.broadcasted_iota(jnp.int32, (STEP, LANES), 1) - lax.broadcasted_iota(
        jnp.int32, (STEP, LANES), 0
    )

    def tile_of(g):
        return (
            pl.ds(g * LANES, LANES),
            pl.ds(pl.multiple_of(offset + g * LANES, LANES), LANES),
        )

    @pl.when(on_diagonal)
    def _():
        preference = 0.25 * levels[...].astype(jnp.float32) - 1.0
        for g in range(groups):
            tile = tile_of(g)
            sim[tile] = jnp.where(eye, preference[g : g + 1, :], sim[tile])

    def lanes_of(k):
        return pl.ds(k * LANES, LANES)

    def rows_at(i):
        return pl.ds(pl.multiple_of(i * STEP, STEP), STEP)

    def top_pass(entry):
        @pl.loop(0, row_count // STEP)
        def _(i):
            here = rows_at(i)
            one = entry(i, here, 0)
            two = jnp.full_like(one, LOWEST)
            for k in range(1, chunks):
                value = entry(i, here, k)
                two = jnp.maximum(two, jnp.minimum(one, value))
                one = jnp.maximum(one, value)
            best[here, :] = one
            second[here, :] = two

    def top_exchange(turn):
        for g in range(groups):
            tile = slice(g * LANES, (g + 1) * LANES)
            one, two = best[tile, :].T, second[tile, :].T
            top = jnp.max(one, axis=0, keepdims=True)
            count = jnp.sum(jnp.where(one == top, 1.0, 0.0), axis=0, keepdims=True)
            rest = jnp.max(
                jnp.maximum(jnp.where(one < top, one, LOWEST), two), axis=0, keepdims=True
            )
            tops[turn, c, g : g + 1, :] = top
            tops[turn, c, groups + g : groups + g + 1, :] = jnp.where(count > 1.0, top, rest)

        def copy(o, slot):
            return pltpu.make_async_remote_copy(
                src_ref=tops.at[turn, c], dst_ref=tops.at[turn, slot],
                send_sem=ts.at[turn, o], recv_sem=tr.at[turn, slot],
                device_id=(r, at_col(o)), device_id_type=MESH,
            )

        for o in range(1, n_col):
            copy(o, c).start()
        for o in range(1, n_col):
            copy(o, at_col(n_col - o)).wait_recv()
        one, two = tops[turn, 0, :groups, :], tops[turn, 0, groups:, :]
        for q in range(1, n_col):
            other, another = tops[turn, q, :groups, :], tops[turn, q, groups:, :]
            two = jnp.maximum(jnp.minimum(one, other), jnp.maximum(two, another))
            one = jnp.maximum(one, other)
        for g in range(groups):
            for ref, value in ((best, one), (second, two)):
                ref[g * LANES : (g + 1) * LANES, :] = jnp.broadcast_to(
                    value[g : g + 1, :], (LANES, LANES)
                ).T
        return lambda: [copy(o, c).wait_send() for o in range(1, n_col)]

    def resp_pass(turn):
        for k in range(chunks):
            lanes = lanes_of(k)

            def body(i, total):
                here = rows_at(i)
                similar = sim[here, lanes]
                combined = similar if turn == 0 else avail[here, lanes] + similar
                fresh = similar - jnp.where(combined >= best[here, :], second[here, :], best[here, :])
                updated = 0.5 * fresh if turn == 0 else 0.5 * resp[here, lanes] + 0.5 * fresh
                resp[here, lanes] = updated
                positive = jnp.where(
                    slant == offset + i * STEP - k * LANES, 0.0, jnp.maximum(updated, 0.0)
                )
                return total + jnp.sum(positive.reshape(STEP // 8, 8, LANES), axis=0)

            total = lax.fori_loop(
                0, row_count // STEP, body, jnp.zeros((8, LANES), jnp.float32), unroll=2
            )
            sums[turn, r, k : k + 1, :] = jnp.sum(total, axis=0, keepdims=True)
        sums[turn, r, chunks:, :] = jnp.zeros((chunks, LANES), jnp.float32)

        @pl.when(on_diagonal)
        def _():
            for g in range(groups):
                sums[turn, r, pl.ds(chunks + offset // LANES + g, 1), :] = jnp.sum(
                    jnp.where(eye, resp[tile_of(g)], 0.0), axis=0, keepdims=True
                )

    def sum_copy(turn, o, slot):
        return pltpu.make_async_remote_copy(
            src_ref=sums.at[turn, r], dst_ref=sums.at[turn, slot],
            send_sem=us.at[turn, o], recv_sem=ur.at[turn, slot],
            device_id=(at_row(o), c), device_id_type=MESH,
        )

    def sum_exchange(turn):
        for o in range(1, n_row):
            sum_copy(turn, o, r).start()
        for o in range(1, n_row):
            sum_copy(turn, o, at_row(n_row - o)).wait_recv()
        total = sums[turn, 0]
        for q in range(1, n_row):
            total = total + sums[turn, q]
        positive = total[:chunks, :]
        return positive, total[chunks:, :] + positive

    def renewed(stats, i, here, k):
        positive, both = stats
        return jnp.where(
            slant == offset + i * STEP - k * LANES,
            positive[k : k + 1, :],
            jnp.minimum(0.0, both[k : k + 1, :] - jnp.maximum(resp[here, lanes_of(k)], 0.0)),
        )

    top_pass(lambda i, here, k: sim[here, lanes_of(k)])
    tops_sent = [top_exchange(0)]
    resp_pass(0)
    stats = sum_exchange(0)

    def second_entry(i, here, k):
        value = 0.5 * renewed(stats, i, here, k)
        avail[here, lanes_of(k)] = value
        return value + sim[here, lanes_of(k)]

    top_pass(second_entry)
    tops_sent.append(top_exchange(1))
    resp_pass(1)
    positive, both = sum_exchange(1)
    final[:chunks, :] = positive
    final[chunks:, :] = both

    for way in (1, -1):

        @pl.when(inside(c + way))
        def _():
            for h in range(PIECES):
                z_own(way, h).wait_send()

        for o in range(1, n_col):
            slot = c - way * o

            @pl.when(inside(slot))
            def _():
                @pl.when(inside(c + way))
                def _():
                    for h in range(PIECES):
                        z_pass(slot, way, h).wait_send()

                target = slot * per + r // n_col

                @pl.when(target != r)
                def _():
                    for h in range(PIECES):
                        row_copy(slot, place, h, target).wait_send()

    for o in range(1, half):
        col_copy(r, cs.at[o], at_row(2 * o)).wait_send()
        col_copy(at_row(n_row - 2 * o), fs.at[o], sibling).wait_send()
    col_copy(r, cs.at[0], sibling).wait_send()
    for sent in tops_sent:
        sent()
    for turn in range(ITERS):
        for o in range(1, n_row):
            sum_copy(turn, o, r).wait_send()


def shards(embeddings, levels):
    n_row, n_col = lax.axis_size("row"), lax.axis_size("col")
    span, width = embeddings.shape
    row_count = levels.shape[0]
    col_count = span * n_row
    groups, chunks = row_count // LANES, col_count // LANES
    full = pltpu.VMEM((row_count, col_count), jnp.float32)
    dma = pltpu.SemaphoreType.DMA
    resp, avail, final = pl.pallas_call(
        functools.partial(kernel, n_row, n_col),
        out_shape=(full, full, pltpu.VMEM((2 * chunks, LANES), jnp.float32)),
        in_specs=[pl.BlockSpec(memory_space=pltpu.HBM)] * 2,
        out_specs=[pl.BlockSpec(memory_space=pltpu.VMEM)] * 3,
        scratch_shapes=[
            pltpu.VMEM((span, width), jnp.float32),
            pltpu.VMEM((groups, LANES), jnp.int32),
            pltpu.VMEM((col_count, width), jnp.float32),
            pltpu.VMEM((n_col, span, width), jnp.float32),
            pltpu.VMEM((row_count, width), jnp.float32),
            pltpu.VMEM((col_count, 3 * width), jnp.bfloat16),
            pltpu.VMEM((row_count, 3 * width), jnp.bfloat16),
            pltpu.VMEM((row_count, col_count), jnp.float32),
            pltpu.VMEM((row_count, LANES), jnp.float32),
            pltpu.VMEM((row_count, LANES), jnp.float32),
            pltpu.VMEM((ITERS, n_col, 2 * groups, LANES), jnp.float32),
            pltpu.VMEM((ITERS, n_row, 2 * chunks, LANES), jnp.float32),
            dma((n_col, PIECES)), dma((n_col, PIECES)), dma((2, PIECES)),
            dma((n_row,)), dma((n_row,)), dma((n_row,)),
            dma((n_col, PIECES)), dma((n_col, PIECES)),
            dma((ITERS, n_col)), dma((ITERS, n_col)),
            dma((ITERS, n_row)), dma((ITERS, n_row)),
            dma, dma((2,)),
        ],
        compiler_params=pltpu.CompilerParams(
            collective_id=0, has_side_effects=True, vmem_limit_bytes=58 * 1024 * 1024 - 8 * row_count * col_count
        ),
        cost_estimate=pl.CostEstimate(
            flops=6 * row_count * col_count * width,
            bytes_accessed=8 * row_count * col_count,
            transcendentals=0,
        ),
    )(embeddings, levels.reshape(groups, LANES))
    row = lax.axis_index("row") * row_count + jnp.arange(row_count, dtype=jnp.int32)
    col = lax.axis_index("col") * col_count + jnp.arange(col_count, dtype=jnp.int32)
    positive = final[:chunks].reshape(1, col_count)
    both = final[chunks:].reshape(1, col_count)
    renewed = jnp.where(
        row[:, None] == col[None, :],
        positive,
        jnp.minimum(0.0, both - jnp.maximum(resp, 0.0)),
    )
    return resp, 0.5 * avail + 0.5 * renewed


def solution(mesh):
    return jax.shard_map(
        shards,
        mesh=mesh,
        in_specs=(P(("col", "row"), None), P("row")),
        out_specs=(P("row", "col"), P("row", "col")),
        check_vma=False,
    )
```

```python
import functools

import jax
import jax.numpy as jnp
from jax import lax
from jax.experimental import pallas as pl
from jax.experimental.pallas import tpu as pltpu
from jax.sharding import PartitionSpec as P

ITERS = 2
LANES = 128
STEP = 32
PIECES = 4
LOWEST = -1e30
MESH = pl.DeviceIdType.MESH


def kernel(
    n_row, n_col, emb_hbm, levels_hbm, resp, avail, final,
    emb, levels, cols, zbuf, rows, cols_cat, rows_cat, sim, best, second, tops, sums,
    zs, zr, zd, cs, cr, fs, rs, rr, ts, tr, us, ur, local, entry,
):
    span, width = emb.shape
    row_count, col_count = sim.shape
    groups, chunks = row_count // LANES, col_count // LANES
    per = n_row // n_col
    r, c = lax.axis_index("row"), lax.axis_index("col")
    sibling = r + 1 - 2 * lax.rem(r, 2)

    def at_row(o):
        return lax.rem(r + o, n_row)

    def at_col(o):
        return lax.rem(c + o, n_col)

    emb_copy = pltpu.make_async_copy(emb_hbm, emb, entry.at[0])
    levels_copy = pltpu.make_async_copy(levels_hbm, levels, entry.at[1])
    emb_copy.start()
    levels_copy.start()
    barrier = pltpu.get_barrier_semaphore()
    for o in range(1, n_row):
        pl.semaphore_signal(barrier, inc=1, device_id=(at_row(o), c), device_id_type=MESH)
    for o in range(1, n_col):
        pl.semaphore_signal(barrier, inc=1, device_id=(r, at_col(o)), device_id_type=MESH)

    def part(index):
        return pl.ds(pl.multiple_of(index * span, span), span)

    emb_copy.wait()
    own = emb[...]
    cols[part(r), :] = own * lax.rsqrt(jnp.sum(own * own, axis=1, keepdims=True) + 1e-06)
    levels_copy.wait()
    pl.semaphore_wait(barrier, n_row + n_col - 2)

    def col_copy(block, send, target):
        return pltpu.make_async_remote_copy(
            src_ref=cols.at[part(block), :], dst_ref=cols.at[part(block), :],
            send_sem=send, recv_sem=cr.at[block], device_id=(target, c), device_id_type=MESH,
        )

    piece = span // PIECES

    def z_copy(source, send, slot, h, target):
        return pltpu.make_async_remote_copy(
            src_ref=source, dst_ref=zbuf.at[slot, pl.ds(h * piece, piece)],
            send_sem=send, recv_sem=zr.at[slot, h], device_id=(r, target), device_id_type=MESH,
        )

    def row_part(place, h):
        return pl.ds(pl.multiple_of(place * span + h * piece, piece), piece)

    def row_copy(slot, place, h, target):
        return pltpu.make_async_remote_copy(
            src_ref=zbuf.at[slot, pl.ds(h * piece, piece)], dst_ref=rows.at[row_part(place, h), :],
            send_sem=rs.at[slot, h], recv_sem=rr.at[place, h],
            device_id=(target, c), device_id_type=MESH,
        )

    half = n_row // 2
    place = lax.rem(r, n_col)

    def z_own(way, h):
        return z_copy(cols.at[row_part(r, h), :], zd.at[(way + 1) // 2, h], c, h, c + way)

    def z_pass(slot, way, h):
        return z_copy(zbuf.at[slot, pl.ds(h * piece, piece)], zs.at[slot, h], slot, h, c + way)

    def inside(index):
        return (index >= 0) & (index < n_col)

    for way in (1, -1):

        @pl.when(inside(c + way))
        def _():
            for h in range(PIECES):
                z_own(way, h).start()

    for o in range(1, half):
        col_copy(r, cs.at[o], at_row(2 * o)).start()
    col_copy(r, cs.at[0], sibling).start()

    def col_step(o):
        source = at_row(n_row - 2 * o)
        col_copy(source, fs.at[o], sibling).wait_recv()
        col_copy(source, fs.at[o], sibling).start()

    for o in range(1, n_col):
        for h in range(PIECES):
            for way in (1, -1):
                slot = c - way * o

                @pl.when(inside(slot))
                def _():
                    z_copy(cols.at[row_part(r, h), :], zs.at[slot, h], slot, h, c).wait_recv()

                    @pl.when(inside(c + way))
                    def _():
                        z_pass(slot, way, h).start()

                    target = slot * per + r // n_col

                    @pl.when(target != r)
                    def _():
                        row_copy(slot, place, h, target).start()

                    @pl.when(target == r)
                    def _():
                        move = pltpu.make_async_copy(
                            zbuf.at[slot, pl.ds(h * piece, piece)],
                            rows.at[row_part(place, h), :],
                            local,
                        )
                        move.start()
                        move.wait()

        if o < half:
            col_step(o)
    for o in range(n_col, half):
        col_step(o)

    col_copy(sibling, cs.at[0], sibling).wait_recv()
    for o in range(1, half):
        col_copy(lax.rem(sibling + n_row - 2 * o, n_row), fs.at[o], sibling).wait_recv()

    def split(ref):
        value = ref[...]
        high = value.astype(jnp.bfloat16)
        return high, (value - high.astype(jnp.float32)).astype(jnp.bfloat16)

    high, low = split(cols)
    cols_cat[:, :width] = high
    cols_cat[:, width : 2 * width] = low
    cols_cat[:, 2 * width :] = high

    source_col = r // per
    first = lax.rem(r, per) * n_col

    @pl.when(source_col == c)
    def _():
        for q in range(n_col):
            rows[q * span : (q + 1) * span, :] = cols[part(first + q), :]

    @pl.when(source_col != c)
    def _():
        for q in range(n_col):

            @pl.when(first + q != r)
            def _():
                for h in range(PIECES):
                    row_copy(c, q, h, sibling).wait_recv()

    high, low = split(rows)
    rows_cat[:, :width] = high
    rows_cat[:, width : 2 * width] = high
    rows_cat[:, 2 * width :] = low

    wide = 2 * LANES

    @pl.loop(0, col_count // wide)
    def _(k):
        lanes = pl.ds(pl.multiple_of(k * wide, wide), wide)
        sim[:, lanes] = lax.dot_general(
            rows_cat[...], cols_cat[lanes, :], (((1,), (1,)), ((), ())),
            preferred_element_type=jnp.float32,
        )

    offset = r * row_count - c * col_count
    on_diagonal = (offset >= 0) & (offset < col_count)
    eye = lax.broadcasted_iota(jnp.int32, (LANES, LANES), 0) == lax.broadcasted_iota(
        jnp.int32, (LANES, LANES), 1
    )
    slant = lax.broadcasted_iota(jnp.int32, (STEP, LANES), 1) - lax.broadcasted_iota(
        jnp.int32, (STEP, LANES), 0
    )

    def tile_of(g):
        return (
            pl.ds(g * LANES, LANES),
            pl.ds(pl.multiple_of(offset + g * LANES, LANES), LANES),
        )

    @pl.when(on_diagonal)
    def _():
        preference = 0.25 * levels[...].astype(jnp.float32) - 1.0
        for g in range(groups):
            tile = tile_of(g)
            sim[tile] = jnp.where(eye, preference[g : g + 1, :], sim[tile])

    def lanes_of(k):
        return pl.ds(k * LANES, LANES)

    def rows_at(i):
        return pl.ds(pl.multiple_of(i * STEP, STEP), STEP)

    def top_pass(entry):
        @pl.loop(0, row_count // STEP)
        def _(i):
            here = rows_at(i)
            one = entry(i, here, 0)
            two = jnp.full_like(one, LOWEST)
            for k in range(1, chunks):
                value = entry(i, here, k)
                two = jnp.maximum(two, jnp.minimum(one, value))
                one = jnp.maximum(one, value)
            best[here, :] = one
            second[here, :] = two

    def top_exchange(turn):
        for g in range(groups):
            tile = slice(g * LANES, (g + 1) * LANES)
            one, two = best[tile, :].T, second[tile, :].T
            top = jnp.max(one, axis=0, keepdims=True)
            count = jnp.sum(jnp.where(one == top, 1.0, 0.0), axis=0, keepdims=True)
            rest = jnp.max(
                jnp.maximum(jnp.where(one < top, one, LOWEST), two), axis=0, keepdims=True
            )
            tops[turn, c, g : g + 1, :] = top
            tops[turn, c, groups + g : groups + g + 1, :] = jnp.where(count > 1.0, top, rest)

        def copy(o, slot):
            return pltpu.make_async_remote_copy(
                src_ref=tops.at[turn, c], dst_ref=tops.at[turn, slot],
                send_sem=ts.at[turn, o], recv_sem=tr.at[turn, slot],
                device_id=(r, at_col(o)), device_id_type=MESH,
            )

        for o in range(1, n_col):
            copy(o, c).start()
        for o in range(1, n_col):
            copy(o, at_col(n_col - o)).wait_recv()
        one, two = tops[turn, 0, :groups, :], tops[turn, 0, groups:, :]
        for q in range(1, n_col):
            other, another = tops[turn, q, :groups, :], tops[turn, q, groups:, :]
            two = jnp.maximum(jnp.minimum(one, other), jnp.maximum(two, another))
            one = jnp.maximum(one, other)
        for g in range(groups):
            for ref, value in ((best, one), (second, two)):
                ref[g * LANES : (g + 1) * LANES, :] = jnp.broadcast_to(
                    value[g : g + 1, :], (LANES, LANES)
                ).T
        return lambda: [copy(o, c).wait_send() for o in range(1, n_col)]

    def resp_pass(turn):
        for k in range(chunks):
            lanes = lanes_of(k)

            def body(i, total):
                here = rows_at(i)
                similar = sim[here, lanes]
                combined = similar if turn == 0 else avail[here, lanes] + similar
                fresh = similar - jnp.where(combined >= best[here, :], second[here, :], best[here, :])
                updated = 0.5 * fresh if turn == 0 else 0.5 * resp[here, lanes] + 0.5 * fresh
                resp[here, lanes] = updated
                positive = jnp.where(
                    slant == offset + i * STEP - k * LANES, 0.0, jnp.maximum(updated, 0.0)
                )
                return total + jnp.sum(positive.reshape(STEP // 8, 8, LANES), axis=0)

            total = lax.fori_loop(
                0, row_count // STEP, body, jnp.zeros((8, LANES), jnp.float32), unroll=8
            )
            sums[turn, r, k : k + 1, :] = jnp.sum(total, axis=0, keepdims=True)
        sums[turn, r, chunks:, :] = jnp.zeros((chunks, LANES), jnp.float32)

        @pl.when(on_diagonal)
        def _():
            for g in range(groups):
                sums[turn, r, pl.ds(chunks + offset // LANES + g, 1), :] = jnp.sum(
                    jnp.where(eye, resp[tile_of(g)], 0.0), axis=0, keepdims=True
                )

    def sum_copy(turn, o, slot):
        return pltpu.make_async_remote_copy(
            src_ref=sums.at[turn, r], dst_ref=sums.at[turn, slot],
            send_sem=us.at[turn, o], recv_sem=ur.at[turn, slot],
            device_id=(at_row(o), c), device_id_type=MESH,
        )

    def sum_exchange(turn):
        for o in range(1, n_row):
            sum_copy(turn, o, r).start()
        for o in range(1, n_row):
            sum_copy(turn, o, at_row(n_row - o)).wait_recv()
        total = sums[turn, 0]
        for q in range(1, n_row):
            total = total + sums[turn, q]
        positive = total[:chunks, :]
        return positive, total[chunks:, :] + positive

    def renewed(stats, i, here, k):
        positive, both = stats
        return jnp.where(
            slant == offset + i * STEP - k * LANES,
            positive[k : k + 1, :],
            jnp.minimum(0.0, both[k : k + 1, :] - jnp.maximum(resp[here, lanes_of(k)], 0.0)),
        )

    top_pass(lambda i, here, k: sim[here, lanes_of(k)])
    tops_sent = [top_exchange(0)]
    resp_pass(0)
    stats = sum_exchange(0)

    def second_entry(i, here, k):
        value = 0.5 * renewed(stats, i, here, k)
        avail[here, lanes_of(k)] = value
        return value + sim[here, lanes_of(k)]

    top_pass(second_entry)
    tops_sent.append(top_exchange(1))
    resp_pass(1)
    positive, both = sum_exchange(1)
    final[:chunks, :] = positive
    final[chunks:, :] = both

    for way in (1, -1):

        @pl.when(inside(c + way))
        def _():
            for h in range(PIECES):
                z_own(way, h).wait_send()

        for o in range(1, n_col):
            slot = c - way * o

            @pl.when(inside(slot))
            def _():
                @pl.when(inside(c + way))
                def _():
                    for h in range(PIECES):
                        z_pass(slot, way, h).wait_send()

                target = slot * per + r // n_col

                @pl.when(target != r)
                def _():
                    for h in range(PIECES):
                        row_copy(slot, place, h, target).wait_send()

    for o in range(1, half):
        col_copy(r, cs.at[o], at_row(2 * o)).wait_send()
        col_copy(at_row(n_row - 2 * o), fs.at[o], sibling).wait_send()
    col_copy(r, cs.at[0], sibling).wait_send()
    for sent in tops_sent:
        sent()
    for turn in range(ITERS):
        for o in range(1, n_row):
            sum_copy(turn, o, r).wait_send()


def finish(offset_ref, resp, avail, final, resp_out, avail_out, held, sems):
    row_count, col_count = resp.shape
    groups, chunks = row_count // LANES, col_count // LANES
    offset = offset_ref[0]
    resp_copy = pltpu.make_async_copy(resp, resp_out, sems.at[groups])
    resp_copy.start()
    slant = lax.broadcasted_iota(jnp.int32, (STEP, LANES), 1) - lax.broadcasted_iota(
        jnp.int32, (STEP, LANES), 0
    )
    copies = []
    for g in range(groups):

        @pl.loop(g * (LANES // STEP), (g + 1) * (LANES // STEP))
        def _(i):
            here = pl.ds(pl.multiple_of(i * STEP, STEP), STEP)
            for k in range(chunks):
                lanes = pl.ds(k * LANES, LANES)
                renewed = jnp.where(
                    slant == offset + i * STEP - k * LANES,
                    final[k : k + 1, :],
                    jnp.minimum(
                        0.0,
                        final[chunks + k : chunks + k + 1, :] - jnp.maximum(resp[here, lanes], 0.0),
                    ),
                )
                held[here, lanes] = 0.5 * avail[here, lanes] + 0.5 * renewed

        piece = pl.ds(g * LANES, LANES)
        copies.append(
            pltpu.make_async_copy(held.at[piece, :], avail_out.at[piece, :], sems.at[g])
        )
        copies[-1].start()
    resp_copy.wait()
    for copy in copies:
        copy.wait()


def shards(embeddings, levels):
    n_row, n_col = lax.axis_size("row"), lax.axis_size("col")
    span, width = embeddings.shape
    row_count = levels.shape[0]
    col_count = span * n_row
    groups, chunks = row_count // LANES, col_count // LANES
    full = pltpu.VMEM((row_count, col_count), jnp.float32)
    dma = pltpu.SemaphoreType.DMA
    resp, avail, final = pl.pallas_call(
        functools.partial(kernel, n_row, n_col),
        out_shape=(full, full, pltpu.VMEM((2 * chunks, LANES), jnp.float32)),
        in_specs=[pl.BlockSpec(memory_space=pltpu.HBM)] * 2,
        out_specs=[pl.BlockSpec(memory_space=pltpu.VMEM)] * 3,
        scratch_shapes=[
            pltpu.VMEM((span, width), jnp.float32),
            pltpu.VMEM((groups, LANES), jnp.int32),
            pltpu.VMEM((col_count, width), jnp.float32),
            pltpu.VMEM((n_col, span, width), jnp.float32),
            pltpu.VMEM((row_count, width), jnp.float32),
            pltpu.VMEM((col_count, 3 * width), jnp.bfloat16),
            pltpu.VMEM((row_count, 3 * width), jnp.bfloat16),
            pltpu.VMEM((row_count, col_count), jnp.float32),
            pltpu.VMEM((row_count, LANES), jnp.float32),
            pltpu.VMEM((row_count, LANES), jnp.float32),
            pltpu.VMEM((ITERS, n_col, 2 * groups, LANES), jnp.float32),
            pltpu.VMEM((ITERS, n_row, 2 * chunks, LANES), jnp.float32),
            dma((n_col, PIECES)), dma((n_col, PIECES)), dma((2, PIECES)),
            dma((n_row,)), dma((n_row,)), dma((n_row,)),
            dma((n_col, PIECES)), dma((n_col, PIECES)),
            dma((ITERS, n_col)), dma((ITERS, n_col)),
            dma((ITERS, n_row)), dma((ITERS, n_row)),
            dma, dma((2,)),
        ],
        compiler_params=pltpu.CompilerParams(
            collective_id=0, has_side_effects=True, vmem_limit_bytes=58 * 1024 * 1024 - 8 * row_count * col_count
        ),
        cost_estimate=pl.CostEstimate(
            flops=6 * row_count * col_count * width,
            bytes_accessed=8 * row_count * col_count,
            transcendentals=0,
        ),
    )(embeddings, levels.reshape(groups, LANES))
    offset = lax.axis_index("row") * row_count - lax.axis_index("col") * col_count
    result = jax.ShapeDtypeStruct((row_count, col_count), jnp.float32)
    return pl.pallas_call(
        finish,
        out_shape=(result, result),
        in_specs=[pl.BlockSpec(memory_space=pltpu.SMEM)]
        + [pl.BlockSpec(memory_space=pltpu.VMEM)] * 3,
        out_specs=[pl.BlockSpec(memory_space=pl.ANY)] * 2,
        scratch_shapes=[pltpu.VMEM((row_count, col_count), jnp.float32), dma((groups + 1,))],
        compiler_params=pltpu.CompilerParams(
            vmem_limit_bytes=4 * row_count * col_count + 4 * 1024 * 1024
        ),
    )(offset.reshape(1), resp, avail, final)


def solution(mesh):
    return jax.shard_map(
        shards,
        mesh=mesh,
        in_specs=(P(("col", "row"), None), P("row")),
        out_specs=(P("row", "col"), P("row", "col")),
        check_vma=False,
    )
```
